32 devices in a mesh: seq: 8 (over y, x, core), dp: 4 (over z).
Axes of the slice: x: 2, y: 2, z: 4, core: 2. Of those that a mesh axis runs over, the one named last changes fastest.
Arguments:
- tokens: bfloat16 [4, 4096, 2048], P('dp', 'seq'), may hold values from -6 to 6
- weights_master: float32 [2048, 3072], P('dp'), may hold values from -0.125 to 0.125
- adam_first: float32 [2048, 3072], P('dp'), may hold values from -6 to 6
- adam_second: float32 [2048, 3072], P('dp'), may hold values from 0.5 to 2
- cotangent: bfloat16 [4, 4096, 1024], P('dp', 'seq'), may hold values from -0.046875 to 0.046875
Outputs:
- attended: bfloat16 [4, 4096, 1024], P('dp', 'seq')
- new_weights: float32 [2048, 3072], P('dp')
- new_first: float32 [2048, 3072], P('dp')
- new_second: float32 [2048, 3072], P('dp')
The draws below stay inside these ranges and needn't reach their ends.
All inputs are finite; a program needn't handle non-finite values.
Results may differ from the reference program's by a relative error of at most 0.0035.
The reference program's roundings to bfloat16 on the way count: a program that leaves them out, or rounds other values in their place, can miss the bound.
Values may be sent and summed in bfloat16 or wider, within the bound.
A program may use at most 128 MiB of HBM per device.

```python
import math
import jax
import jax.numpy as jnp
from jax import lax

D = 2048
HEADS = 8
HDIM = 128
TOK_DEV = 512
BLOCK = 512
STEP = 100
TOKENS = 4096
SEQS = 4
N_SEQ = 8


def spiked(values, rng, source, target, shards_of, factor):
    def block_of(position):
        return (jnp.arange(values.shape[position]) // (values.shape[position] // shards_of)).reshape((-1,) + (1,) * (values.ndim - 1 - position))

    one_side = jax.random.permutation(rng, shards_of)[block_of(target)]
    second = (block_of(target) + shards_of // 2) % shards_of
    return jnp.where((block_of(source) == one_side) | (block_of(source) == second), factor * values, values)


def levels(key, dims, cuts, least, largest):
    level, own = 1.0, jax.random.fold_in(key, 6)
    for dim, blocks in cuts:
        draws = jnp.exp(jax.random.uniform(jax.random.fold_in(own, dim), (blocks,), jnp.float32, least / len(cuts), largest / len(cuts)))
        level = level * jnp.repeat(draws, dims[dim] // blocks).reshape([-1 if axis == dim else 1 for axis in range(len(dims))])
    return level


def centred(key, shape, scale, reach, cuts=(), held_as=jnp.bfloat16):
    array = jax.random.normal(key, shape, jnp.float32) * scale
    if len(cuts) > 0:
        array = levels(key, shape, cuts, -0.22, 0.18) * array
    return jnp.clip(array, min=-reach, max=reach).astype(held_as)


def bell_draw_with(stream_key, shape, spread, reach, shards, heavy, kind=jnp.bfloat16):
    drawn = spread * jax.random.normal(stream_key, shape, jnp.float32)
    if shards:
        drawn = drawn * levels(stream_key, shape, shards, -0.22, 0.18)
    return jnp.clip(spiked(drawn, jax.random.fold_in(stream_key, 3), *heavy), -reach, reach).astype(kind)


def setup_inputs(seed: int = 0) -> dict:
    streams_of = jax.random.split(jax.random.key(seed), 6)
    tokens = bell_draw_with(streams_of[0], (SEQS, TOKENS, D), 1.0, 6.0, ((0, 4), (1, 8)), (0, 2, 4, 2.0))
    weights_master = centred(streams_of[1], (D, 3 * HEADS * HDIM), D ** -0.5, 0.125, ((0, 4),), jnp.float32)
    adam_first = centred(streams_of[2], (D, 3 * HEADS * HDIM), 1.0, 6.0, ((0, 4),), jnp.float32)
    adam_second = jnp.clip(jnp.exp(math.log(2.0) - 1.3862944 * jax.random.uniform(streams_of[3], (D, 3 * HEADS * HDIM), jnp.float32) ** levels(streams_of[3], (D, 3 * HEADS * HDIM), ((0, 4),), -0.2, 0.2)), 0.5, 2.0)
    cotangent = centred(streams_of[4], (SEQS, TOKENS, HEADS * HDIM), (TOKENS * SEQS) ** -0.5, 0.046875, ((0, 4), (1, 8)))
    return dict(tokens=tokens, weights_master=weights_master, adam_first=adam_first, adam_second=adam_second, cotangent=cotangent)


EPS_NORM = 1e-05
BETA_ONE = 0.9
BETA_TWO = 0.95
LEARN_RATE = 0.001
DECAY_WEIGHT = 0.1
EPS_ADAM = 1e-08

def causal_table():
    places = jnp.arange(BLOCK, dtype=jnp.int32)
    return places[:, None] >= places[None, :]

def block_scores(query_block, key_block):
    causal = causal_table()
    scores = jnp.einsum('the,she->hts', query_block.astype(jnp.float32), key_block.astype(jnp.float32))
    return jnp.where(causal[None], scores, 0.0).astype(jnp.bfloat16)

def forward_block(operands):
    query_block, key_block, value_block, carried_state = operands
    scores = block_scores(query_block, key_block)
    within = jnp.einsum('hts,she->the', scores.astype(jnp.float32), value_block.astype(jnp.float32))
    carried = jnp.einsum('the,hef->thf', query_block.astype(jnp.float32), carried_state.astype(jnp.float32))
    return within + carried

def backward_block(operands):
    query_block, key_block, value_block, grad_block, carried_state, later_state = operands
    causal = causal_table()
    scores = block_scores(query_block, key_block)
    back = jnp.einsum('thf,shf->hts', grad_block.astype(jnp.float32), value_block.astype(jnp.float32))
    back = jnp.where(causal[None], back, 0.0).astype(jnp.bfloat16)
    query_f = query_block.astype(jnp.float32)
    key_f = key_block.astype(jnp.float32)
    value_f = value_block.astype(jnp.float32)
    grad_f = grad_block.astype(jnp.float32)
    carried_f = carried_state.astype(jnp.float32)
    later_f = later_state.astype(jnp.float32)
    back_f = back.astype(jnp.float32)
    scores_f = scores.astype(jnp.float32)
    grad_query = jnp.einsum('hts,she->the', back_f, key_f) + jnp.einsum('thf,hef->the', grad_f, carried_f)
    grad_key = jnp.einsum('hts,the->she', back_f, query_f) + jnp.einsum('shf,hef->she', value_f, later_f)
    grad_value = jnp.einsum('hts,thf->shf', scores_f, grad_f) + jnp.einsum('she,hef->shf', key_f, later_f)
    inner_width = HEADS * HDIM
    joined = jnp.concatenate([grad_query.reshape(BLOCK, inner_width), grad_key.reshape(BLOCK, inner_width), grad_value.reshape(BLOCK, inner_width)], axis=1)
    return joined.astype(jnp.bfloat16)

def sequence_pass(tokens_seq, weights_bf, cotangent_seq):
    blocks = TOKENS // BLOCK
    inner_width = HEADS * HDIM
    qkv = jnp.dot(tokens_seq, weights_bf, preferred_element_type=jnp.float32).astype(jnp.bfloat16)
    queries = qkv[:, :inner_width].reshape(blocks, BLOCK, HEADS, HDIM)
    key_heads = qkv[:, inner_width:2 * inner_width].reshape(blocks, BLOCK, HEADS, HDIM)
    value_heads = qkv[:, 2 * inner_width:].reshape(blocks, BLOCK, HEADS, HDIM)
    kv_local = jnp.einsum('bshe,bshf->bhef', key_heads.astype(jnp.float32), value_heads.astype(jnp.float32))
    prefix_state = (jnp.cumsum(kv_local, 0) - kv_local).astype(jnp.bfloat16)
    mixed = lax.map(forward_block, (queries, key_heads, value_heads, prefix_state))
    inverse_rms = lax.rsqrt(lax.optimization_barrier(jnp.mean(mixed * mixed, -1, keepdims=True)) + EPS_NORM)
    normed = mixed * inverse_rms
    attended_seq = normed.astype(jnp.bfloat16).reshape(TOKENS, inner_width)
    grad_out = cotangent_seq.astype(jnp.float32).reshape(blocks, BLOCK, HEADS, HDIM)
    along = lax.optimization_barrier(jnp.mean(grad_out * normed, -1, keepdims=True))
    grad_mixed = (inverse_rms * (grad_out - normed * along)).astype(jnp.bfloat16)
    qg_local = jnp.einsum('bthe,bthf->bhef', queries.astype(jnp.float32), grad_mixed.astype(jnp.float32))
    suffix_state = (jnp.cumsum(qg_local[::-1], 0)[::-1] - qg_local).astype(jnp.bfloat16)
    grad_qkv = lax.map(backward_block, (queries, key_heads, value_heads, grad_mixed, prefix_state, suffix_state))
    return (attended_seq, grad_qkv.reshape(TOKENS, 3 * inner_width))

def reference(tokens, weights_master, adam_first, adam_second, cotangent):
    weights_bf = weights_master.astype(jnp.bfloat16)

    def one_sequence(running, operands):
        tokens_seq, cotangent_seq = operands
        attended_seq, grad_qkv = sequence_pass(tokens_seq, weights_bf, cotangent_seq)
        device_tokens = tokens_seq.reshape(N_SEQ, TOK_DEV, D)
        device_grads = grad_qkv.reshape(N_SEQ, TOK_DEV, grad_qkv.shape[1])

        def add_device(total, pieces):
            token_rows, grad_rows = pieces
            partial_value = jnp.dot(token_rows.T, grad_rows, preferred_element_type=jnp.float32).astype(jnp.bfloat16)
            partial_value = lax.optimization_barrier(partial_value)
            return (total + partial_value.astype(jnp.float32), None)
        running, unused = lax.scan(add_device, running, (device_tokens, device_grads))
        return (running, attended_seq)
    gradient, attended = lax.scan(one_sequence, jnp.zeros(weights_master.shape, jnp.float32), (tokens, cotangent))
    new_first = BETA_ONE * adam_first + (1.0 - BETA_ONE) * gradient
    new_second = BETA_TWO * adam_second + (1.0 - BETA_TWO) * gradient * gradient
    first_hat = new_first / (1.0 - BETA_ONE ** STEP)
    second_hat = new_second / (1.0 - BETA_TWO ** STEP)
    new_weights = weights_master - LEARN_RATE * (first_hat / (jnp.sqrt(second_hat) + EPS_ADAM) + DECAY_WEIGHT * weights_master)
    return (attended, new_weights, new_first, new_second)
```

```python
import functools

import jax
import jax.numpy as jnp
from jax import lax
from jax.experimental import pallas as pl
from jax.experimental.pallas import tpu as pltpu
from jax.sharding import PartitionSpec as P

HDIM = 128
BLOCK = 512
STEP = 100


EPS_NORM = 1e-05
BETA_ONE = 0.9
BETA_TWO = 0.95
LEARN_RATE = 0.001
DECAY_WEIGHT = 0.1
EPS_ADAM = 1e-08


def causal_table():
    places = jnp.arange(BLOCK, dtype=jnp.int32)
    return places[:, None] >= places[None, :]


def block_scores(query_block, key_block):
    causal = causal_table()
    scores = jnp.einsum("the,she->hts", query_block, key_block, preferred_element_type=jnp.float32)
    return jnp.where(causal[None], scores, 0.0).astype(jnp.bfloat16)


def forward_block(operands):
    query_block, key_block, value_block, carried_state = operands
    scores = block_scores(query_block, key_block)
    within = jnp.einsum("hts,she->the", scores, value_block, preferred_element_type=jnp.float32)
    carried = jnp.einsum(
        "the,hef->thf", query_block, carried_state, preferred_element_type=jnp.float32
    )
    return within + carried


def backward_block(operands):
    query_block, key_block, value_block, grad_block, carried_state, later_state = operands
    causal = causal_table()
    scores = block_scores(query_block, key_block)
    back = jnp.einsum("thf,shf->hts", grad_block, value_block, preferred_element_type=jnp.float32)
    back = jnp.where(causal[None], back, 0.0).astype(jnp.bfloat16)
    grad_query = jnp.einsum("hts,she->the", back, key_block, preferred_element_type=jnp.float32)
    grad_query = grad_query + jnp.einsum(
        "thf,hef->the", grad_block, carried_state, preferred_element_type=jnp.float32
    )
    grad_key = jnp.einsum("hts,the->she", back, query_block, preferred_element_type=jnp.float32)
    grad_key = grad_key + jnp.einsum(
        "shf,hef->she", value_block, later_state, preferred_element_type=jnp.float32
    )
    grad_value = jnp.einsum("hts,thf->shf", scores, grad_block, preferred_element_type=jnp.float32)
    grad_value = grad_value + jnp.einsum(
        "she,hef->shf", key_block, later_state, preferred_element_type=jnp.float32
    )
    block_rows = query_block.shape[0]
    joined = jnp.concatenate(
        [
            grad_query.reshape(block_rows, -1),
            grad_key.reshape(block_rows, -1),
            grad_value.reshape(block_rows, -1),
        ],
        axis=1,
    )
    return joined.astype(jnp.bfloat16)


def adam_step(weights_master, adam_first, adam_second, gradient):
    new_first = BETA_ONE * adam_first + (1.0 - BETA_ONE) * gradient
    new_second = BETA_TWO * adam_second + (1.0 - BETA_TWO) * gradient * gradient
    first_hat = new_first / (1.0 - BETA_ONE**STEP)
    second_hat = new_second / (1.0 - BETA_TWO**STEP)
    new_weights = weights_master - LEARN_RATE * (
        first_hat / (jnp.sqrt(second_hat) + EPS_ADAM) + DECAY_WEIGHT * weights_master
    )
    return new_weights, new_first, new_second


def token_split(tokens, weights_master, adam_first, adam_second, cotangent):
    inputs = tokens[0]
    row_total = inputs.shape[0]
    model_dim = inputs.shape[1]
    inner_width = cotangent.shape[2]
    head_count = inner_width // HDIM
    blocks = row_total // BLOCK
    triple = 3 * inner_width
    position = lax.axis_index("seq")
    weights_bf = weights_master.astype(jnp.bfloat16)
    columns = inputs
    projected = jnp.dot(
        columns,
        lax.all_gather(weights_bf, "dp", axis=0, tiled=True),
        preferred_element_type=jnp.float32,
    )
    qkv = projected.astype(jnp.bfloat16)
    queries = qkv[:, :inner_width].reshape(blocks, BLOCK, head_count, HDIM)
    key_heads = qkv[:, inner_width : 2 * inner_width].reshape(blocks, BLOCK, head_count, HDIM)
    value_heads = qkv[:, 2 * inner_width :].reshape(blocks, BLOCK, head_count, HDIM)
    kv_local = jnp.einsum(
        "bshe,bshf->bhef", key_heads, value_heads, preferred_element_type=jnp.float32
    )
    kv_total = jnp.sum(kv_local, 0)
    state_zeros = jnp.zeros(kv_total.shape, jnp.float32)
    incoming = lax.all_gather(kv_total[None], "seq", axis=0, tiled=True)
    owners = jnp.arange(incoming.shape[0], dtype=jnp.int32)
    kept = jnp.where((owners < position)[:, None, None, None], incoming, 0.0)
    kv_before = jnp.sum(kept, 0)
    prefix_state = (kv_before[None] + (jnp.cumsum(kv_local, 0) - kv_local)).astype(jnp.bfloat16)
    mixed = lax.map(forward_block, (queries, key_heads, value_heads, prefix_state))
    inverse_rms = lax.rsqrt(jnp.mean(mixed * mixed, -1, keepdims=True) + EPS_NORM)
    normed = mixed * inverse_rms
    attended = normed.astype(jnp.bfloat16).reshape(1, row_total, inner_width)
    grad_out = cotangent[0].astype(jnp.float32).reshape(blocks, BLOCK, head_count, HDIM)
    along = jnp.mean(grad_out * normed, -1, keepdims=True)
    grad_mixed = (inverse_rms * (grad_out - normed * along)).astype(jnp.bfloat16)
    qg_local = jnp.einsum(
        "bthe,bthf->bhef", queries, grad_mixed, preferred_element_type=jnp.float32
    )
    qg_total = jnp.sum(qg_local, 0)
    incoming = lax.all_gather(
        qg_total[None].astype(jnp.bfloat16), "seq", axis=0, tiled=True
    ).astype(jnp.float32)
    owners = jnp.arange(incoming.shape[0], dtype=jnp.int32)
    kept = jnp.where((owners > position)[:, None, None, None], incoming, 0.0)
    qg_after = state_zeros + jnp.sum(kept, 0)
    suffix_state = (qg_after[None] + (jnp.cumsum(qg_local[::-1], 0)[::-1] - qg_local)).astype(
        jnp.bfloat16
    )
    grad_qkv = lax.map(
        backward_block, (queries, key_heads, value_heads, grad_mixed, prefix_state, suffix_state)
    )
    grad_qkv = grad_qkv.reshape(row_total, triple)
    seq_count = lax.axis_size("seq")
    dp_count = lax.axis_size("dp")
    piece_rows = model_dim // (seq_count * dp_count)
    reordered = inputs.reshape(row_total, dp_count, seq_count, piece_rows)
    reordered = jnp.transpose(reordered, (0, 2, 1, 3)).reshape(row_total, model_dim)
    columns = reordered
    partial_value = jnp.einsum(
        "td,tc->dc", columns, grad_qkv, preferred_element_type=jnp.float32
    ).astype(jnp.bfloat16)
    partial_value = lax.optimization_barrier(partial_value)
    summed = lax.psum_scatter(
        partial_value.astype(jnp.float32), ("seq", "dp"), scatter_dimension=0, tiled=True
    )
    gradient = lax.all_gather(summed.astype(jnp.bfloat16), "seq", axis=0, tiled=True).astype(
        summed.dtype
    )
    return (attended,) + adam_step(weights_master, adam_first, adam_second, gradient)


CHUNKS = 4


def mm(left, right, dims):
    return lax.dot_general(left, right, (dims, ((), ())), preferred_element_type=jnp.float32)


NN = ((1,), (0,))
NT = ((1,), (1,))
TN = ((0,), (0,))


def head_kernel(
    dp_count,
    tokens_ref,
    weights_ref,
    cot_ref,
    att_out,
    grad_out,
    tok,
    w_stage,
    w_bf,
    cot,
    qkv,
    scores,
    prefix,
    att,
    grad_mixed,
    grad_t,
    part,
    part_in,
    total,
    gathered,
    state,
    local_sem,
    tok_recv,
    tok_send,
    relay_send,
    twin_send,
    w_recv,
    w_send,
    cot_recv,
    cot_send,
    att_recv,
    att_send,
    part_recv,
    part_send,
    sum_recv,
    sum_send,
):
    me = lax.axis_index("seq")
    row = lax.axis_index("dp")
    depth = weights_ref.shape[0]
    heads = 8
    inner = heads * HDIM
    width = 3 * HDIM
    side = 1 - 2 * (me % 2)
    step_x = 2 - 4 * ((me // 2) % 2)
    step_y = 4 - 8 * (me // 4)
    twin = me + side
    near_x = me + step_x
    near_y = me + step_y
    far = me + step_x + step_y
    others = [
        me + step_x + step_y + side,
        far,
        near_x + side,
        near_y + side,
        near_x,
        near_y,
        twin,
    ]
    size = BLOCK // CHUNKS

    def block(index):
        return pl.ds(pl.multiple_of(index * BLOCK, BLOCK), BLOCK)

    def piece(index, chunk):
        return pl.ds(pl.multiple_of(index * BLOCK + chunk * size, size), size)

    def head_cols(index, part_index):
        return pl.ds(pl.multiple_of(part_index * inner + index * HDIM, HDIM), HDIM)

    def remote(src, dst, send, recv, **axis):
        return pltpu.make_async_remote_copy(
            src_ref=src,
            dst_ref=dst,
            send_sem=send,
            recv_sem=recv,
            device_id=axis,
            device_id_type=pl.DeviceIdType.MESH,
        )

    fetch = [
        pltpu.make_async_copy(
            weights_ref.at[:, head_cols(me, i)],
            w_stage.at[:, pl.ds(i * HDIM, HDIM)],
            local_sem.at[i],
        )
        for i in range(3)
    ]
    for copy in fetch:
        copy.start()
    own_tok = pltpu.make_async_copy(tokens_ref, tok.at[block(me), :], local_sem.at[3])
    own_tok.start()
    own_cot = pltpu.make_async_copy(
        cot_ref.at[:, head_cols(me, 0)], cot.at[block(me), :], local_sem.at[4]
    )
    own_cot.start()

    barrier = pltpu.get_barrier_semaphore()
    for other in others:
        pl.semaphore_signal(
            barrier, inc=1, device_id={"seq": other}, device_id_type=pl.DeviceIdType.MESH
        )
    for r in range(1, dp_count):
        pl.semaphore_signal(
            barrier,
            inc=1,
            device_id={"dp": (row + r) % dp_count},
            device_id_type=pl.DeviceIdType.MESH,
        )
    pl.semaphore_wait(barrier, len(others) + dp_count - 1)

    waits = []

    def send(copy):
        copy.start()
        waits.append(copy)

    def own_piece(chunk, slot, target):
        send(
            remote(
                tokens_ref.at[pl.ds(chunk * size, size), :],
                tok.at[piece(me, chunk), :],
                tok_send.at[slot, chunk],
                tok_recv.at[me, chunk],
                seq=target,
            )
        )

    x_order = [0, 1, 2, 3]
    y_order = [2, 3, 0, 1]
    for t in range(CHUNKS):
        own_piece(x_order[t], 0, near_x)
        own_piece(y_order[t], 1, near_y)
    for t in range(CHUNKS):
        own_piece(t, 2, twin)

    for copy in fetch:
        copy.wait()
    own_rows = pl.ds(pl.multiple_of(row * depth, depth), depth)
    w_bf[own_rows, :] = w_stage[...].astype(jnp.bfloat16)
    for r in range(1, dp_count):
        send(
            remote(
                w_bf.at[own_rows, :],
                w_bf.at[own_rows, :],
                w_send.at[r],
                w_recv.at[row],
                dp=(row + r) % dp_count,
            )
        )

    def arrived(source, chunk):
        place = tok.at[piece(source, chunk), :]
        remote(place, place, tok_send.at[0, 0], tok_recv.at[source, chunk], seq=twin).wait_recv()

    def pass_on(source, chunk, send_sem, target):
        place = tok.at[piece(source, chunk), :]
        send(remote(place, place, send_sem, tok_recv.at[source, chunk], seq=target))

    def project(source):
        qkv[block(source), :] = mm(tok[block(source), :], w_bf[...], NN).astype(jnp.bfloat16)

    for t in range(CHUNKS):
        arrived(near_x, x_order[t])
        if t < CHUNKS // 2:
            pass_on(near_x, x_order[t], relay_send.at[0, t], near_y)
        arrived(near_y, y_order[t])
        if t < CHUNKS // 2:
            pass_on(near_y, y_order[t], relay_send.at[1, t], near_x)
        pass_on(near_x, x_order[t], twin_send.at[0, t], twin)
        pass_on(near_y, y_order[t], twin_send.at[1, t], twin)
    for r in range(1, dp_count):
        source = (row + dp_count - r) % dp_count
        rows = w_bf.at[pl.ds(pl.multiple_of(source * depth, depth), depth), :]
        remote(rows, rows, w_send.at[r], w_recv.at[source], dp=source).wait_recv()
    own_tok.wait()
    for t in range(CHUNKS):
        arrived(twin, t)
    project(me)
    project(twin)
    for t in range(CHUNKS // 2):
        arrived(far, x_order[t])
        arrived(far, y_order[t])
        pass_on(far, x_order[t], twin_send.at[2, 2 * t], twin)
        pass_on(far, y_order[t], twin_send.at[2, 2 * t + 1], twin)
        if t == 0:
            for k, other in enumerate(others):
                send(
                    remote(
                        cot_ref.at[:, head_cols(other, 0)],
                        cot.at[block(me), :],
                        cot_send.at[k],
                        cot_recv.at[me],
                        seq=other,
                    )
                )
            project(near_x)
            project(near_y)
            for source in (near_x + side, near_y + side):
                for chunk in range(CHUNKS):
                    arrived(source, chunk)
                project(source)
    project(far)
    for chunk in range(CHUNKS):
        arrived(far + side, chunk)
    project(far + side)
    own_cot.wait()
    for other in others:
        place = cot.at[block(other), :]
        remote(place, place, cot_send.at[0], cot_recv.at[other], seq=other).wait_recv()

    causal = lax.broadcasted_iota(jnp.int32, (BLOCK, BLOCK), 0) >= lax.broadcasted_iota(
        jnp.int32, (BLOCK, BLOCK), 1
    )
    state[...] = jnp.zeros_like(state)

    def forward(b, carry):
        rows = block(b)
        query = qkv[rows, 0:HDIM]
        key = qkv[rows, HDIM : 2 * HDIM]
        value = qkv[rows, 2 * HDIM : width]
        before = state[...].astype(jnp.bfloat16)
        prefix[b] = before
        table = jnp.where(causal, mm(query, key, NT), 0.0).astype(jnp.bfloat16)
        scores[rows, :] = table
        mixed = mm(table, value, NN) + mm(query, before, NN)
        inverse_rms = lax.rsqrt(jnp.mean(mixed * mixed, -1, keepdims=True) + EPS_NORM)
        normed = mixed * inverse_rms
        att[rows, :] = normed.astype(jnp.bfloat16)
        given = cot[rows, :].astype(jnp.float32)
        along = jnp.mean(given * normed, -1, keepdims=True)
        grad_mixed[rows, :] = (inverse_rms * (given - normed * along)).astype(jnp.bfloat16)
        state[...] += mm(key, value, TN)
        return carry

    lax.fori_loop(0, heads, forward, 0)

    own_att = pltpu.make_async_copy(
        att.at[block(me), :], att_out.at[:, head_cols(me, 0)], local_sem.at[5]
    )
    own_att.start()
    for k, other in enumerate(others):
        send(
            remote(
                att.at[block(other), :],
                att_out.at[:, head_cols(me, 0)],
                att_send.at[k],
                att_recv.at[me],
                seq=other,
            )
        )

    state[...] = jnp.zeros_like(state)

    def backward(step, carry):
        rows = block(heads - 1 - step)
        query = qkv[rows, 0:HDIM]
        key = qkv[rows, HDIM : 2 * HDIM]
        value = qkv[rows, 2 * HDIM : width]
        grad = grad_mixed[rows, :]
        later = state[...].astype(jnp.bfloat16)
        before = prefix[heads - 1 - step]
        table = scores[rows, :]
        back = jnp.where(causal, mm(grad, value, NT), 0.0).astype(jnp.bfloat16)
        grad_query = mm(back, key, NN) + mm(grad, before, NT)
        grad_key = mm(back, query, TN) + mm(value, later, NT)
        grad_value = mm(table, grad, TN) + mm(key, later, NN)
        grad_t[0:HDIM, rows] = grad_query.T.astype(jnp.bfloat16)
        grad_t[HDIM : 2 * HDIM, rows] = grad_key.T.astype(jnp.bfloat16)
        grad_t[2 * HDIM : width, rows] = grad_value.T.astype(jnp.bfloat16)
        state[...] += mm(query, grad, TN)
        return carry

    lax.fori_loop(0, heads, backward, 0)

    def partial_sum(target):
        columns = pl.ds(pl.multiple_of(target * depth, depth), depth)
        gathered[...] = jnp.zeros_like(gathered)

        def add_block(b, carry):
            rows = block(b)
            share = mm(grad_t[:, rows], tok[rows, columns], NN)
            gathered[...] += share.astype(jnp.bfloat16).astype(jnp.float32)
            return carry

        lax.fori_loop(0, heads, add_block, 0)
        return gathered[...]

    for r in range(1, dp_count):
        target = (row + r) % dp_count
        part[r] = partial_sum(target).astype(jnp.bfloat16)
        send(remote(part.at[r], part_in.at[row], part_send.at[r], part_recv.at[row], dp=target))
    summed = partial_sum(row)
    for r in range(1, dp_count):
        source = (row + dp_count - r) % dp_count
        place = part_in.at[source]
        remote(place, place, part_send.at[r], part_recv.at[source], dp=source).wait_recv()
        summed = summed + part_in[source].astype(jnp.float32)
    total[...] = summed.T

    own_sum = []
    for i in range(3):
        piece_cols = total.at[:, pl.ds(i * HDIM, HDIM)]
        for k, other in enumerate((near_x, near_y, far, twin)):
            send(
                remote(
                    piece_cols,
                    grad_out.at[:, head_cols(me, i)],
                    sum_send.at[k, i],
                    sum_recv.at[me, i],
                    seq=other,
                )
            )
        own_sum.append(
            pltpu.make_async_copy(
                piece_cols, grad_out.at[:, head_cols(me, i)], local_sem.at[6 + i]
            )
        )
        own_sum[i].start()

    def sum_arrived(source, i):
        place = grad_out.at[:, head_cols(source, i)]
        remote(place, place, sum_send.at[0, 0], sum_recv.at[source, i], seq=twin).wait_recv()

    for k, source in enumerate((near_x, near_y, far)):
        for i in range(3):
            sum_arrived(source, i)
            place = grad_out.at[:, head_cols(source, i)]
            send(remote(place, place, sum_send.at[4 + k, i], sum_recv.at[source, i], seq=twin))
    for source in (twin, near_x + side, near_y + side, far + side):
        for i in range(3):
            sum_arrived(source, i)
    for other in others:
        place = att_out.at[:, head_cols(other, 0)]
        remote(place, place, att_send.at[0], att_recv.at[other], seq=other).wait_recv()
    own_att.wait()
    for copy in own_sum:
        copy.wait()
    for copy in waits:
        copy.wait_send()


def head_split(tokens, weights_master, adam_first, adam_second, cotangent):
    inputs = tokens[0]
    model_dim = inputs.shape[1]
    depth = weights_master.shape[0]
    seq_count = lax.axis_size("seq")
    dp_count = lax.axis_size("dp")
    total_rows = seq_count * BLOCK
    width = 3 * HDIM
    anywhere = pl.BlockSpec(memory_space=pl.ANY)
    dma = pltpu.SemaphoreType.DMA
    attended, gradient = pl.pallas_call(
        functools.partial(head_kernel, dp_count),
        out_shape=(
            jax.ShapeDtypeStruct((BLOCK, cotangent.shape[2]), jnp.bfloat16),
            jax.ShapeDtypeStruct(weights_master.shape, jnp.float32),
        ),
        in_specs=[anywhere] * 3,
        out_specs=(anywhere, anywhere),
        scratch_shapes=[
            pltpu.VMEM((total_rows, model_dim), jnp.bfloat16),
            pltpu.VMEM((depth, width), jnp.float32),
            pltpu.VMEM((model_dim, width), jnp.bfloat16),
            pltpu.VMEM((total_rows, HDIM), jnp.bfloat16),
            pltpu.VMEM((total_rows, width), jnp.bfloat16),
            pltpu.VMEM((total_rows, BLOCK), jnp.bfloat16),
            pltpu.VMEM((seq_count, HDIM, HDIM), jnp.bfloat16),
            pltpu.VMEM((total_rows, HDIM), jnp.bfloat16),
            pltpu.VMEM((total_rows, HDIM), jnp.bfloat16),
            pltpu.VMEM((width, total_rows), jnp.bfloat16),
            pltpu.VMEM((dp_count, width, depth), jnp.bfloat16),
            pltpu.VMEM((dp_count, width, depth), jnp.bfloat16),
            pltpu.VMEM((depth, width), jnp.float32),
            pltpu.VMEM((width, depth), jnp.float32),
            pltpu.VMEM((HDIM, HDIM), jnp.float32),
            dma((9,)),
            dma((seq_count, CHUNKS)),
            dma((3, CHUNKS)),
            dma((2, CHUNKS // 2)),
            dma((3, CHUNKS)),
            dma((dp_count,)),
            dma((dp_count,)),
            dma((seq_count,)),
            dma((seq_count,)),
            dma((seq_count,)),
            dma((seq_count,)),
            dma((dp_count,)),
            dma((dp_count,)),
            dma((seq_count, 3)),
            dma((7, 3)),
        ],
        compiler_params=pltpu.CompilerParams(
            collective_id=0, has_side_effects=True, vmem_limit_bytes=56 * 1024 * 1024
        ),
        cost_estimate=pl.CostEstimate(
            flops=18 * 10**9, bytes_accessed=64 * 2**20, transcendentals=0
        ),
    )(inputs, weights_master, cotangent[0])
    return (attended[None],) + adam_step(
        weights_master, adam_first, adam_second, gradient
    )


def solution(mesh):
    placed = (
        P("dp", "seq", None),
        P("dp", None),
        P("dp", None),
        P("dp", None),
        P("dp", "seq", None),
    )

    def local(tokens, weights_master, adam_first, adam_second, cotangent):
        heads = cotangent.shape[2] // HDIM
        one_head_each = mesh.shape["seq"] == heads == 8 and tokens.shape[1] == BLOCK
        form = head_split if one_head_each else token_split
        return form(tokens, weights_master, adam_first, adam_second, cotangent)

    return jax.shard_map(
        local,
        mesh=mesh,
        in_specs=placed,
        out_specs=(P("dp", "seq", None), P("dp", None), P("dp", None), P("dp", None)),
        check_vma=False,
    )
```
